256 devices in a mesh: dp: 8 (over x, core), expert: 32 (over y, z).
Axes of the slice: x: 4, y: 4, z: 8, core: 2. Of those that a mesh axis runs over, the one named last changes fastest.
Arguments:
- grad_values: bfloat16 [32768, 4096], P(('dp', 'expert')), may hold values from -6 to 6
- grad_exponents: int32 [32768, 32], P(('dp', 'expert')), may hold values from -6 to 4
- routes: int32 [32768, 8], P(('dp', 'expert')), may hold values from 0 to 31, all different within a row; in each aligned block of 128 rows (0 to 127, 128 to 255, ...) at most 36 rows name the same one
- gates: bfloat16 [32768, 8], P(('dp', 'expert')), may hold values from 0.019897461 to 0.29882812
- saved_pre: bfloat16 [8, 32, 32, 36, 1536], P('dp', None, 'expert'), may hold values from -6 to 6
- down_weight: bfloat16 [32, 768, 4096], P('expert', 'dp')
Outputs:
- gate_grad: float32 [32768, 8], P(('dp', 'expert'))
- grad_pre: bfloat16 [8, 32, 32, 36, 1536], P('dp', None, 'expert')
- weight_grad: float32 [32, 4096, 768], P('expert', 'dp')
The draws below stay inside these ranges and needn't reach their ends.
Inputs may be any that keep to these rules, and one draw needn't show every extreme that they name: `routes`: the rows of one device name each expert at most 36 times.
All inputs are finite; a program needn't handle non-finite values.
Results may differ from the reference program's by a relative error of at most 0.0065.
Values may be sent and summed in bfloat16 or wider, within the bound.
No kernel may reach another device: no remote copies, remote signals or barrier semaphores. Data moves between devices by JAX's collectives and lax.ppermute only.
A program may use at most 128 MiB of HBM per device.

```python
import math
import jax
import jax.numpy as jnp
import numpy as np
from jax import lax

D = 4096
HW = 768
TOP = 8
BLK = 128
TOK_DEV = 128
EXPERTS = 32
TOKENS = 32768
CAP = 36
N_DP = 8
N_EXPERT = 32


def draw_grad_exponents(key, part):
    key = jax.random.fold_in(key, 11)
    first, second = jax.random.split(key, 2)
    count = D // BLK
    order = jax.random.permutation(first, count).astype(jnp.int32)
    base = -5 + order * 9 // count
    jitter = jax.random.randint(second, (TOKENS, count), -1, 2).astype(jnp.int32)
    jitter = jitter.at[0].set(-1).at[1].set(1)
    return (base[None, :] + jitter).astype(jnp.int32)


def draw_down_weight(key, part):
    key = jax.random.fold_in(key, 23)
    first, second = jax.random.split(key, 2)
    columns = jnp.exp(jax.random.uniform(first, (EXPERTS, 1, D), minval=math.log(0.5), maxval=math.log(5.0)))
    values = jax.random.truncated_normal(second, -4.0, 4.0, (EXPERTS, HW, D))
    return (values * columns / math.sqrt(HW)).astype(jnp.bfloat16)


def shard_levels(own_key, dims, cuts, low, largest):
    def one(axis_at, shards_of):
        draws = jax.random.uniform(jax.random.fold_in(jax.random.fold_in(own_key, 6), axis_at), (shards_of,), jnp.float32, low / len(cuts), largest / len(cuts))
        return jnp.repeat(jnp.exp(draws), dims[axis_at] // shards_of).reshape((-1,) + (1,) * (len(dims) - axis_at - 1))

    factor_of = one(*cuts[0])
    for cut in cuts[1:]:
        factor_of = factor_of * one(*cut)
    return factor_of


def routed_block(stream_key, own, number, rows, number_of, top, reach, slope):
    sequence = jax.random.permutation(stream_key, number_of)
    heavy_load, common = shares(number_of, rows * top, reach, slope, True), shares(number_of, rows * top, reach, slope, False)
    places = jnp.arange(number_of)

    def named(sizes, rotation):
        used = int((sizes > 0).sum())
        fixed = max(1, used // 4)
        shifted = fixed + (places - fixed + rotation * (used - fixed)) % max(1, number_of - fixed)
        return jnp.zeros((number_of,), jnp.int32).at[sequence[jnp.where(places < fixed, places, shifted)]].set(jnp.asarray(sizes, jnp.int32))

    sizes = jnp.where(number % 4 == 0, named(heavy_load, number // 4), named(common, number - number // 4 - 1))
    mixed = jax.random.permutation(jax.random.fold_in(own, 3), number_of)
    donor, receiver = mixed[0:number_of // 2 * 2:2], mixed[1:number_of // 2 * 2:2]
    margin = jnp.minimum(sizes[donor] - 1, reach - sizes[receiver]) // 2
    margin = jnp.where((donor == sequence[0]) | (receiver == sequence[0]) | (sizes[receiver] == 0), 0, jnp.maximum(margin, 0))
    shifted = jax.random.randint(jax.random.fold_in(own, 4), (number_of // 2,), 0, 1 << 20) % (margin + 1)
    sizes = sizes.at[donor].add(-shifted).at[receiver].add(shifted)
    labels = jnp.searchsorted(jnp.cumsum(sizes), jnp.arange(rows * top), side="right").astype(jnp.int32)
    table = labels.reshape(top, rows).T
    table = table[jax.random.permutation(jax.random.fold_in(own, 1), rows)]
    rotation = jax.random.randint(jax.random.fold_in(own, 2), (rows, 1), 0, top)
    return jnp.take_along_axis(table, (jnp.arange(top)[None, :] + rotation) % top, axis=1)


def shares(count, total, bound, slope, full):
    loads = [(1 << 20) // math.isqrt(rank ** slope) + 1 for rank in range(1, count + 1)]
    largest = bound if full else min(bound, max(-(-total // count), total * loads[0] // sum(loads)))
    least = 1 if total - largest >= count - 1 else 0
    given, surplus = [largest] + [least] * (count - 1), total - largest - least * (count - 1)
    while surplus > 0:
        free = [i for i in range(1, count) if given[i] < largest] or [i for i in range(1, count) if given[i] < bound]
        mass, left = sum([loads[i] for i in free]), surplus
        for i in free:
            addition = min(bound - given[i], max(1, left * loads[i] // mass), surplus)
            given[i] = given[i] + addition
            surplus = surplus - addition
    return np.array(given)


def noise(key, shape, width, bound, cuts=(), kind=jnp.bfloat16):
    values = jax.random.normal(key, shape, jnp.float32) * width
    if len(cuts) > 0:
        values = shard_levels(key, shape, cuts, -0.22, 0.18) * values
    return jnp.clip(values, min=-bound, max=bound).astype(kind)


def setup_inputs(seed: int = 0) -> dict:
    splits = jax.random.split(jax.random.key(seed), 7)
    grad_values = noise(splits[0], (TOKENS, D), 1.0, 6.0, ((0, 256),))
    grad_exponents = draw_grad_exponents(jax.random.fold_in(splits[6], 71), 0)
    routes_keys = jax.random.split(jax.random.fold_in(splits[2], 1), TOKENS // TOK_DEV)
    routes_turns = jax.random.permutation(jax.random.fold_in(splits[2], 3), TOKENS // TOK_DEV)
    routes = jax.vmap(lambda own, number: routed_block(jax.random.fold_in(splits[2], 2), own, number, TOK_DEV, EXPERTS, TOP, CAP, 2))(routes_keys, routes_turns).reshape((TOKENS, TOP))
    gates = jnp.clip(jnp.exp(math.log(0.29882812) - 2.7092764 * jax.random.uniform(splits[3], (TOKENS, TOP), jnp.float32) ** shard_levels(splits[3], (TOKENS, TOP), ((0, 256),), -0.2, 0.2)), 0.019897461, 0.29882812).astype(jnp.bfloat16)
    saved_pre = noise(splits[4], (N_DP, N_EXPERT, EXPERTS, CAP, 2 * HW), 1.5, 6.0, ((0, 8), (2, 32)))
    down_weight = draw_down_weight(jax.random.fold_in(splits[6], 71), 0)
    return {"grad_values": grad_values, "grad_exponents": grad_exponents, "routes": routes, "gates": gates, "saved_pre": saved_pre, "down_weight": down_weight}


limit = 16.0
epsilon = 1e-06

def silu_pieces(pre):
    sigmoid = jax.nn.sigmoid(pre)
    return (pre * sigmoid, sigmoid * (1.0 + pre * (1.0 - sigmoid)))

def reference(grad_values, grad_exponents, routes, gates, saved_pre, down_weight):
    groups = N_DP * N_EXPERT
    per_group = TOK_DEV * TOP
    blocks = D // BLK
    scales = jnp.exp2(grad_exponents.astype(jnp.float32))
    scaled = (grad_values.astype(jnp.float32).reshape(TOKENS, blocks, BLK) * scales[:, :, None]).reshape(TOKENS, D).astype(jnp.bfloat16)
    chosen = routes.reshape(groups, per_group)
    onehot = (chosen[:, :, None] == jnp.arange(EXPERTS, dtype=jnp.int32)[None, None, :]).astype(jnp.int32)
    before = lax.optimization_barrier(jnp.sum((jnp.cumsum(onehot, axis=1) - onehot) * onehot, axis=2)).astype(jnp.int32)
    group_index = jnp.arange(groups, dtype=jnp.int32)[:, None]
    position = ((group_index * EXPERTS + chosen) * CAP + before).astype(jnp.int32)
    route_count = TOKENS * TOP
    filler = jnp.full((groups * EXPERTS * CAP,), route_count, jnp.int32)
    slot_route = filler.at[position.reshape(-1)].set(jnp.arange(route_count, dtype=jnp.int32)).reshape(groups, EXPERTS, CAP)
    padded_rows = jnp.concatenate([scaled, jnp.zeros((1, D), jnp.bfloat16)], axis=0)
    padded_gates = jnp.concatenate([gates.reshape(-1), jnp.zeros((1,), jnp.bfloat16)])
    stored_all = saved_pre.reshape(groups, EXPERTS, CAP, 2 * HW)

    def per_expert(expert_id):
        slots = lax.dynamic_index_in_dim(slot_route, expert_id, 1, keepdims=False).reshape(groups * CAP)
        received = padded_rows[slots // TOP]
        weights_in = padded_gates[slots].astype(jnp.float32)[:, None]
        weight = lax.dynamic_index_in_dim(down_weight, expert_id, 0, keepdims=False)
        product = jnp.dot(received, weight.T, preferred_element_type=jnp.float32)
        stored = lax.dynamic_index_in_dim(stored_all, expert_id, 1, keepdims=False).reshape(groups * CAP, 2 * HW).astype(jnp.float32)
        gate_pre = stored[:, :HW]
        up_pre = stored[:, HW:]
        silu_value, silu_slope = silu_pieces(gate_pre)
        activation = silu_value * up_pre
        gate_slots = lax.optimization_barrier(jnp.sum(product * activation, axis=1))
        scaled_grad = weights_in * product
        grad_out = jnp.concatenate([scaled_grad * up_pre * silu_slope, scaled_grad * silu_value], axis=1).astype(jnp.bfloat16)
        weighted = (weights_in * activation).astype(jnp.bfloat16)
        summed = jnp.dot(received.T, weighted, preferred_element_type=jnp.float32)
        own_weight = weight.astype(jnp.float32)
        weight_sq = lax.optimization_barrier(jnp.sum(own_weight * own_weight, axis=0))
        grad_sq = lax.optimization_barrier(jnp.sum(summed * summed, axis=1))
        ratio = jnp.minimum(1.0, limit * jnp.sqrt(weight_sq + epsilon) / jnp.sqrt(grad_sq + epsilon))
        return (gate_slots.reshape(groups, CAP), grad_out.reshape(groups, CAP, 2 * HW), summed * ratio[:, None])
    gate_slots, grad_slots, weight_grad = lax.map(per_expert, jnp.arange(EXPERTS, dtype=jnp.int32))
    gate_grad = gate_slots[chosen, group_index, before].reshape(TOKENS, TOP)
    grad_pre = jnp.moveaxis(grad_slots, 0, 1).reshape(N_DP, N_EXPERT, EXPERTS, CAP, 2 * HW)
    return (gate_grad, grad_pre, weight_grad)
```

```python
import jax
import jax.numpy as jnp
import numpy as np
from jax import lax
from jax.experimental import pallas as pl
from jax.experimental.pallas import tpu as pltpu
from jax.sharding import Mesh
from jax.sharding import PartitionSpec as P

LIMIT = 16.0
EPS = 1e-06
BF = jnp.bfloat16
F32 = jnp.float32
I32 = jnp.int32
OFFSETS = (0, 1, -1, 2, -2, 3, -3, 4)
MIB = 1024 * 1024


def params(mib, **kw):
    return pltpu.CompilerParams(vmem_limit_bytes=max(mib, 56) * MIB, **kw)


def cost(flops, size):
    return pl.CostEstimate(flops=1000, bytes_accessed=1000, transcendentals=0)


def shift(a, axis, size, by):
    return lax.ppermute(a, axis, [(i, (i + by) % size) for i in range(size)])


def scale_kernel(groups, quarters, lanes, gv_ref, ge_ref, *outs):
    scales = jnp.exp2(ge_ref[...].astype(F32))
    for out, (first, count) in zip(outs, groups):
        for n in range(count):
            for i in range(lanes // 128):
                block = i * quarters + first + n
                vals = gv_ref[:, block * 128 : block * 128 + 128].astype(F32)
                out[n, :, i * 128 : i * 128 + 128] = (vals * scales[:, block : block + 1]).astype(BF)


def scale_tokens(gv, ge, groups, quarters):
    rows, width = gv.shape
    lanes = width // quarters
    return pl.pallas_call(
        lambda *refs: scale_kernel(groups, quarters, lanes, *refs),
        out_shape=[jax.ShapeDtypeStruct((count, rows, lanes), BF) for _, count in groups],
        compiler_params=params(16),
        cost_estimate=cost(rows * width, 4 * rows * width),
        name="scale",
    )(gv, ge)


def strict_upper(n):
    return (lax.broadcasted_iota(I32, (n, n), 0) < lax.broadcasted_iota(I32, (n, n), 1)).astype(BF)


def hits(routes, expert):
    hit = (routes == expert.astype(F32)).astype(F32)
    return hit


def selector_kernel(dests, zsize, cap, info_ref, meta_ref, out_ref):
    toks = meta_ref.shape[2]
    upper = strict_upper(toks)
    y, z = info_ref[0], info_ref[1]
    slot = lax.broadcasted_iota(I32, (cap, zsize, toks), 0).astype(F32)
    owner = lax.broadcasted_iota(I32, (cap, zsize, toks), 1)

    def piece(p, _):
        group = (z + info_ref[2 + p]) % zsize
        routes = meta_ref[y * zsize + group].astype(F32)[0:8]
        for d in range(dests):
            mask = jnp.max(hits(routes, ((y + d) % dests) * zsize + z), axis=0, keepdims=True)
            mask8 = jnp.broadcast_to(mask, (8, toks))
            rank = jnp.dot(mask8.astype(BF), upper, preferred_element_type=F32)
            place = jnp.where(mask8 > 0.5, rank, -1.0)[0:1]
            chosen = jnp.where((slot == place[None]) & (owner == group), 1.0, 0.0)
            out_ref[d, :, pl.ds(pl.multiple_of(p * toks, 128), toks)] = chosen.reshape(cap * zsize, toks).astype(BF)
        return 0

    lax.fori_loop(0, zsize, piece, 0)


def selector(info, meta, dests, zsize, cap):
    toks = meta.shape[2]
    return pl.pallas_call(
        lambda *refs: selector_kernel(dests, zsize, cap, *refs),
        out_shape=jax.ShapeDtypeStruct((dests, cap * zsize, zsize * toks), BF),
        in_specs=[pl.BlockSpec(memory_space=pltpu.SMEM), pl.BlockSpec(memory_space=pltpu.VMEM)],
        compiler_params=params(24),
        cost_estimate=cost(8e6, 3e6),
        name="selector",
    )(info, meta)


def gather_kernel(dests, sel_ref, *refs):
    pieces, outs, held = refs[: -1 - dests], refs[-1 - dests : -1], refs[-1]
    toks = pieces[0].shape[1]
    for p, ref in enumerate(pieces):
        held[p * toks : p * toks + toks, :] = ref[0]
    made = jnp.dot(sel_ref[...], held[...], preferred_element_type=F32).astype(BF)
    rows = outs[0].shape[0]
    for d in range(dests):
        outs[d][...] = made[d * rows : d * rows + rows]


def gather_slots(sel, pieces, places):
    dests, rows, depth = sel.shape
    _, toks, lanes = pieces[0].shape
    return pl.pallas_call(
        lambda *refs: gather_kernel(dests, *refs),
        grid=(lanes // 256,),
        out_shape=[jax.ShapeDtypeStruct((rows, lanes), BF)] * dests,
        in_specs=[pl.BlockSpec((dests * rows, depth), lambda n: (0, 0))]
        + [pl.BlockSpec((1, toks, 256), lambda n, at=at: (at, 0, n)) for at in places],
        out_specs=[pl.BlockSpec((rows, 256), lambda n: (0, n))] * dests,
        scratch_shapes=[pltpu.VMEM((depth, 256), BF)],
        compiler_params=params(16),
        cost_estimate=cost(2 * dests * rows * depth * lanes, 2 * dests * rows * (depth + lanes) + 2 * depth * lanes),
        name="gather",
    )(sel.reshape(dests * rows, depth), *pieces)


def slot_pieces(meta, expert, upper):
    routes, gates = meta[:, 0:8], meta[:, 8:16]
    hit = (routes == expert.astype(F32)).astype(F32)
    mask = jnp.max(hit, axis=1)
    gate = jnp.sum(hit * gates, axis=1)
    rank = jnp.dot(mask.astype(BF), upper, preferred_element_type=F32)
    return jnp.where(mask > 0.5, rank, -1.0), gate


def slot_weight(place, gate, r):
    return jnp.sum(jnp.where(place == r.astype(F32), gate, 0.0), axis=1, keepdims=True)


def weighted_kernel(cap, zsize, hidden, info_ref, meta_ref, pre_ref, out_ref, held):
    pair = pl.program_id(0)
    rows = cap * zsize
    expert = info_ref[0] * zsize + info_ref[1]
    upper = strict_upper(meta_ref.shape[2])
    found = [slot_pieces(meta_ref[half * zsize : half * zsize + zsize].astype(F32), expert, upper) for half in range(2)]

    def step(r, _):
        pre = pre_ref[r].astype(F32)
        for half in range(2):
            p = pre[half * zsize : half * zsize + zsize, :hidden]
            q = pre[half * zsize : half * zsize + zsize, hidden:]
            act = p * jax.nn.sigmoid(p) * q
            w = slot_weight(found[half][0], found[half][1], r)
            at = pl.multiple_of((pair * 2 + half) * rows + r * zsize, 8)
            held[pl.ds(at, zsize), :] = w * act
        return 0

    lax.fori_loop(0, cap, step, 0, unroll=6)

    @pl.when(pair == pl.num_programs(0) - 1)
    def _():
        for c in range(hidden // 128):
            out_ref[c * 128 : c * 128 + 128, :] = held[:, c * 128 : c * 128 + 128].T.astype(BF)


def weighted_t(info, meta, pre, zsize):
    cap, groups, both = pre.shape
    hidden = both // 2
    steps = groups // (2 * zsize)
    return pl.pallas_call(
        lambda *refs: weighted_kernel(cap, zsize, hidden, *refs),
        grid=(steps,),
        out_shape=jax.ShapeDtypeStruct((hidden, cap * groups), BF),
        in_specs=[
            pl.BlockSpec(memory_space=pltpu.SMEM),
            pl.BlockSpec((2 * zsize,) + meta.shape[1:], lambda g: (g, 0, 0)),
            pl.BlockSpec((cap, 2 * zsize, both), lambda g: (0, g, 0)),
        ],
        out_specs=pl.BlockSpec((hidden, cap * groups), lambda g: (0, 0)),
        scratch_shapes=[pltpu.VMEM((cap * groups, hidden), F32)],
        compiler_params=params(24),
        cost_estimate=cost(20e6, 6e6),
        name="weighted",
    )(info, meta, pre)


def rec_copies(info_ref, recs, held, sem):
    dests = len(recs)
    rows = recs[0].shape[0]
    copies = []
    for j, ref in enumerate(recs):
        at = pl.multiple_of(((info_ref[0] + dests - j) % dests) * rows, 16)
        copies.append(pltpu.make_async_copy(ref, held.at[pl.ds(at, rows)], sem.at[j]))
    return copies


def weight_copies(quarters, quarter, w_ref, held, sem):
    return [
        pltpu.make_async_copy(
            w_ref.at[:, pl.ds((i * quarters + quarter) * 128, 128)], held.at[:, pl.ds(i * 128, 128)], sem.at[i]
        )
        for i in range(held.shape[1] // 128)
    ]


def run_copies(copies):
    for c in copies:
        c.start()
    for c in copies:
        c.wait()


def nt(a, b):
    return lax.dot_general(a, b, (((1,), (1,)), ((), ())), preferred_element_type=F32)


def sum_kernel(count, dests, per, with_product, more, info_ref, wt_ref, *refs):
    recs, refs = refs[: count * dests], refs[count * dests :]
    held = refs[-1]
    step = pl.program_id(0)
    rows = recs[0].shape[0]
    for n in range(count):

        @pl.when(step // per == n)
        def _(n=n):
            for j in range(dests):
                at = pl.multiple_of(((info_ref[0] + dests - j) % dests) * rows, 16)
                held[pl.ds(at, rows), :] = recs[n * dests + j][...]

    if with_product:
        low_ref, high_ref = refs[:2]
        out_ref, prod_ref = refs[2 + more : 4 + more]
        weights = jnp.concatenate([low_ref[...], high_ref[...]], axis=1)

        @pl.when(step == 0)
        def _():
            prod_ref[...] = refs[2][...] if more else jnp.zeros_like(prod_ref)

        prod_ref[...] += nt(held[...], weights)
    else:
        out_ref = refs[0]
    out = jnp.dot(wt_ref[...], held[...], preferred_element_type=F32).astype(out_ref.dtype)
    out_ref[0, 0] = out[:, :128]
    out_ref[1, 0] = out[:, 128:]


def partial_sum(info, wt, recs, kind, w=None, first=0, quarters=4, before=None):
    hidden, rows = wt.shape
    count, dests = len(recs), len(recs[0])
    size, lanes = recs[0][0].shape
    per = lanes // 256
    with_product, more = w is not None, int(before is not None)
    whole = pl.BlockSpec((rows, hidden), lambda n: (0, 0))
    in_specs = [pl.BlockSpec(memory_space=pltpu.SMEM), pl.BlockSpec((hidden, rows), lambda n: (0, 0))]
    for m in range(count):
        in_specs += [pl.BlockSpec((size, 256), lambda n, m=m: (0, jnp.clip(n - m * per, 0, per - 1)))] * dests
    out_specs = [pl.BlockSpec((2, 1, hidden, 128), lambda n: (n % per, n // per, 0, 0))]
    out_shape = [jax.ShapeDtypeStruct((lanes // 128, count, hidden, 128), kind)]
    args = [info, wt] + sum(recs, [])
    if with_product:
        for k in range(2):
            in_specs.append(
                pl.BlockSpec((hidden, 128), lambda n, k=k: (0, ((n % per) * 2 + k) * quarters + first + n // per))
            )
        args += [w, w]
        if more:
            in_specs.append(whole)
            args.append(before)
        out_specs.append(whole)
        out_shape.append(jax.ShapeDtypeStruct((rows, hidden), F32))
    return pl.pallas_call(
        lambda *refs: sum_kernel(count, dests, per, with_product, more, *refs),
        grid=(count * per,),
        out_shape=out_shape,
        in_specs=in_specs,
        out_specs=out_specs,
        scratch_shapes=[pltpu.VMEM((rows, 256), BF)],
        compiler_params=params(48),
        cost_estimate=cost(2 * hidden * rows * lanes, 2 * (hidden * rows + rows * lanes + hidden * lanes)),
        name="partial_sum",
    )(*args)


def rec_copies(info_ref, recs, held, sem):
    dests = len(recs)
    rows = recs[0].shape[0]
    copies = []
    for j, ref in enumerate(recs):
        at = pl.multiple_of(((info_ref[0] + dests - j) % dests) * rows, 16)
        copies.append(pltpu.make_async_copy(ref, held.at[pl.ds(at, rows)], sem.at[j]))
    return copies


def weight_copies(quarters, quarter, w_ref, held, sem):
    return [
        pltpu.make_async_copy(
            w_ref.at[:, pl.ds((i * quarters + quarter) * 128, 128)], held.at[:, pl.ds(i * 128, 128)], sem.at[i]
        )
        for i in range(held.shape[1] // 128)
    ]


def run_copies(copies):
    for c in copies:
        c.start()
    for c in copies:
        c.wait()


def finish_kernel(cap, zsize, hidden, quarters, quarter, dests, *refs):
    info_ref, meta_ref, pre_ref, prod_ref = refs[:4]
    recs = refs[4 : 4 + dests]
    w_ref, grad_ref, gate_ref, held, weights, total, sem, w_sem = refs[4 + dests :]

    @pl.when(pl.program_id(0) == 0)
    def _():
        run_copies(rec_copies(info_ref, recs, held, sem) + weight_copies(quarters, quarter, w_ref, weights, w_sem))

    size = total.shape[0]
    at = pl.multiple_of(pl.program_id(0) * size, 16)
    total[...] = prod_ref[...] + nt(held[pl.ds(at, size), :], weights[...])

    rows = cap * zsize
    toks = meta_ref.shape[2]
    expert = info_ref[0] * zsize + info_ref[1]
    upper = strict_upper(toks)
    found = [slot_pieces(meta_ref[half * zsize : half * zsize + zsize].astype(F32), expert, upper) for half in range(2)]
    lane = lax.broadcasted_iota(I32, (zsize, 128), 1)

    def step(r, gates):
        pre = pre_ref[r].astype(F32)
        grads, kept = [], []
        for half in range(2):
            p = pre[half * zsize : half * zsize + zsize, :hidden]
            q = pre[half * zsize : half * zsize + zsize, hidden:]
            sg = jax.nn.sigmoid(p)
            silu = p * sg
            w = slot_weight(found[half][0], found[half][1], r)
            prod = total[pl.ds(pl.multiple_of(half * rows + r * zsize, 8), zsize), :]
            gate = jnp.sum(prod * (silu * q), axis=1, keepdims=True)
            h = w * prod
            grads.append(jnp.concatenate([h * q * (sg * (1.0 + p * (1.0 - sg))), h * silu], axis=1))
            kept.append(jnp.where(lane == r, gate, gates[half]))
        grad_ref[r] = jnp.concatenate(grads, axis=0).astype(BF)
        return tuple(kept)

    zero = jnp.zeros((zsize, 128), F32)
    gates = lax.fori_loop(0, cap, step, (zero, zero), unroll=6)
    gate_ref[0:zsize] = gates[0]
    gate_ref[zsize : 2 * zsize] = gates[1]


def finish(info, meta, pre, prod, recs, w, quarter, quarters, zsize):
    cap, groups, both = pre.shape
    hidden = both // 2
    rows, lanes = recs[0].shape
    dests = len(recs)
    steps = groups // (2 * zsize)
    size = rows * dests // steps
    return pl.pallas_call(
        lambda *refs: finish_kernel(cap, zsize, hidden, quarters, quarter, dests, *refs),
        grid=(steps,),
        out_shape=[jax.ShapeDtypeStruct(pre.shape, BF), jax.ShapeDtypeStruct((groups, 128), F32)],
        in_specs=[
            pl.BlockSpec(memory_space=pltpu.SMEM),
            pl.BlockSpec((2 * zsize,) + meta.shape[1:], lambda g: (g, 0, 0)),
            pl.BlockSpec((cap, 2 * zsize, both), lambda g: (0, g, 0)),
            pl.BlockSpec((size, hidden), lambda g: (g, 0)),
        ]
        + [pl.BlockSpec(memory_space=pl.ANY)] * (dests + 1),
        out_specs=[
            pl.BlockSpec((cap, 2 * zsize, both), lambda g: (0, g, 0)),
            pl.BlockSpec((2 * zsize, 128), lambda g: (g, 0)),
        ],
        scratch_shapes=[
            pltpu.VMEM((rows * dests, lanes), BF),
            pltpu.VMEM((hidden, lanes), BF),
            pltpu.VMEM((size, hidden), F32),
            pltpu.SemaphoreType.DMA((dests,)),
            pltpu.SemaphoreType.DMA((lanes // 128,)),
        ],
        compiler_params=params(40),
        cost_estimate=cost(2 * rows * lanes * hidden + 30e6, 20e6),
        name="finish",
    )(info, meta, pre, prod, *recs, w)


def clip_kernel(parts, info_ref, *refs):
    part_ref, w_ref, out_ref = refs[0], refs[1], refs[-1]
    total = part_ref[0, 0].astype(F32)
    for i in range(1, parts):
        total += part_ref[i, 0].astype(F32)
    own = w_ref[...].astype(F32)
    weight_sq = jnp.sum(own * own, axis=0, keepdims=True)
    grad_sq = jnp.sum(total * total, axis=0, keepdims=True)
    ratio = jnp.minimum(1.0, LIMIT * jnp.sqrt(weight_sq + EPS) / jnp.sqrt(grad_sq + EPS))
    out_ref[...] = (total * ratio).T


def clipped(where, parts, w, first, quarters, before):
    count, num, hidden, lanes = parts.shape
    specs = [
        pl.BlockSpec((count, 1, hidden, lanes), lambda g, info: (0, g, 0, 0)),
        pl.BlockSpec((hidden, lanes), lambda g, info: (0, info[0] * quarters + first + g)),
    ]
    args = [where, parts, w]
    aliases = {}
    if before is not None:
        specs.append(pl.BlockSpec(memory_space=pl.ANY))
        args.append(before)
        aliases = {3: 0}
    return pl.pallas_call(
        lambda *refs: clip_kernel(count, *refs),
        grid_spec=pltpu.PrefetchScalarGridSpec(
            num_scalar_prefetch=1,
            grid=(num,),
            in_specs=specs,
            out_specs=pl.BlockSpec((lanes, hidden), lambda g, info: (first + g, 0)),
        ),
        out_shape=jax.ShapeDtypeStruct((lanes * quarters, hidden), F32),
        input_output_aliases=aliases,
        compiler_params=params(16),
        cost_estimate=cost(2e6, 2.5e6),
        name="clip",
    )(*args)


def gate_kernel(routes_ref, back_ref, out_ref):
    toks, fanout = routes_ref.shape
    experts = back_ref.shape[0]
    expert = lax.broadcasted_iota(I32, (toks, experts), 1)
    hit = [(routes_ref[:, k : k + 1] == expert).astype(F32) for k in range(fanout)]
    anyhit = hit[0]
    for k in range(1, fanout):
        anyhit += hit[k]
    lower = (lax.broadcasted_iota(I32, (toks, toks), 0) > lax.broadcasted_iota(I32, (toks, toks), 1)).astype(BF)
    before = jnp.dot(lower, anyhit.astype(BF), preferred_element_type=F32)
    slot = lax.broadcasted_iota(I32, (toks, 128), 1).astype(F32)
    for k in range(fanout):
        rank = jnp.sum(hit[k] * before, axis=1, keepdims=True)
        vals = jnp.dot(hit[k], back_ref[...], preferred_element_type=F32, precision=lax.Precision.HIGHEST)
        out_ref[:, k : k + 1] = jnp.sum(jnp.where(slot == rank, vals, 0.0), axis=1, keepdims=True)


def gate_select(routes, back):
    return pl.pallas_call(
        gate_kernel,
        out_shape=jax.ShapeDtypeStruct(routes.shape, F32),
        compiler_params=params(16),
        cost_estimate=cost(40e6, 2e5),
        name="gate",
    )(routes, back)


def body(sizes, grad_values, grad_exponents, routes, gates, saved_pre, down_weight):
    xs, cs, ys, zs = sizes
    quarters = 4
    cap = saved_pre.shape[3]
    toks = routes.shape[0]
    y, z = lax.axis_index("y"), lax.axis_index("z")
    dp = lax.axis_index("x") * cs + lax.axis_index("c")
    info = jnp.concatenate([jnp.stack([y, z]).astype(I32), jnp.array([-k % zs for k in OFFSETS], I32)])
    where = jnp.stack([dp]).astype(I32)

    meta = jnp.concatenate([routes.T.astype(BF), gates.T], axis=0)
    meta = lax.all_gather(meta, ("y", "z"), axis=0)
    groups = ((0, 1), (1, 1), (2, 2))
    chunks = scale_tokens(grad_values, grad_exponents, groups, quarters)

    one = lax.optimization_barrier
    pre = jnp.transpose(saved_pre[0, :, 0], (1, 0, 2))

    def to_slots(q):
        return list(gather_slots(sel, *pieces[q]))

    def move(sent, *by):
        return [shift(sent[d], "y", ys, d) for d in by]

    def across(parts):
        return lax.all_to_all(parts, ("x", "c"), split_axis=0, concat_axis=0, tiled=True)

    def scatter(parts):
        return lax.psum_scatter(parts, ("x", "c"), scatter_dimension=0, tiled=True)

    def in_order(own, got):
        return [own, got[0], got[2], got[1]]

    pieces = {}
    ahead, back = list(chunks[:2]), list(chunks[:2])
    got = [[c] for c in chunks[:2]]
    for s in range(3):
        ahead = [shift(a, "z", zs, 1) for a in ahead]
        back = [shift(b, "z", zs, -1) for b in back]
        if s < 2:
            ahead, back = one((ahead, back))
        else:
            ahead, back, meta, own, shard = one((ahead, back, meta, chunks[2], down_weight[0]))
            sel = selector(info, meta, ys, zs, cap)
        for g, a, b in zip(got, ahead, back):
            g += [a, b]
    w = lax.all_gather(shard, ("x", "c"), axis=0, tiled=True)
    last = [shift(ahead[0], "z", zs, 1), shift(back[1], "z", zs, -1)]
    ahead, back = shift(own, "z", zs, 1), shift(own, "z", zs, -1)
    last, sel, meta = one((last, sel, meta))
    for q in range(2):
        pieces[q] = (got[q] + [last[q]], [0] * 8)

    first = to_slots(0)
    first_got = move(first, 1, 3)
    ahead, back, first_got, first, meta = one((ahead, back, first_got, first, meta))
    got = [own, ahead, back]

    ahead, back = shift(ahead, "z", zs, 1), shift(back, "z", zs, -1)
    first_got += move(first, 2)
    second = to_slots(1)
    wt = weighted_t(info, meta, pre, zs)
    ahead, back, first_got, second, wt = one((ahead, back, first_got, second, wt))
    got += [ahead, back]
    rec = in_order(first[0], first_got)

    ahead, back = shift(ahead, "z", zs, 1), shift(back, "z", zs, -1)
    second_got = move(second, 1, 3)
    parts, prod = partial_sum(info, wt, [rec], BF, w, 0, quarters)
    ahead, back, second_got, second, parts, prod = one((ahead, back, second_got, second, parts, prod))
    got += [ahead, back]

    parts0 = scatter(parts)
    last = [shift(ahead[:1], "z", zs, 1), shift(back[1:], "z", zs, -1)]
    second_got += move(second, 2)
    last, second_got = one((last, second_got))
    pieces[2] = (got + last[:1], [0] * 8)
    pieces[3] = (got + last[1:], [1] * 7 + [0])
    rec = in_order(second[0], second_got)

    first = to_slots(2)
    first_got = move(first, 1, 3)
    parts, prod = partial_sum(info, wt, [rec], BF, w, 1, quarters, prod)
    first_got, first, parts, prod = one((first_got, first, parts, prod))

    parts1 = scatter(parts)
    first_got += move(first, 2)
    second = to_slots(3)
    first_got, second = one((first_got, second))
    rec = in_order(first[0], first_got)

    second_got = move(second, 1, 3)
    parts, prod = partial_sum(info, wt, [rec], BF, w, 2, quarters, prod)
    second_got, second, parts, prod = one((second_got, second, parts, prod))

    parts2 = across(parts)
    second_got += move(second, 2)
    grads = clipped(where, parts0, w, 0, quarters, None)
    second_got, grads, parts2 = one((second_got, grads, parts2))
    rec = in_order(second[0], second_got)

    (parts,) = partial_sum(info, wt, [rec], BF)
    parts3 = scatter(parts)
    grad_pre, gate_slots = finish(info, meta, pre, prod, rec, w, 3, quarters, zs)
    back = lax.all_to_all(gate_slots, ("y", "z"), split_axis=0, concat_axis=0, tiled=True)
    grads = clipped(where, parts1, w, 1, quarters, grads)
    grads = clipped(where, parts2, w, 2, quarters, grads)
    gate_grad = gate_select(routes, back)
    grads = clipped(where, parts3, w, 3, quarters, grads)
    grad_pre = jnp.transpose(grad_pre, (1, 0, 2))[None, :, None]
    return gate_grad, grad_pre, grads[None]


def solution(mesh):
    sizes = (4, 2, 4, 8)
    fine = Mesh(mesh.devices.reshape(sizes), ("x", "c", "y", "z"))
    dp, ex = ("x", "c"), ("y", "z")
    tok = P(dp + ex, None)
    return jax.shard_map(
        lambda *args: body(sizes, *args),
        mesh=fine,
        in_specs=(tok, tok, tok, tok, P(dp, None, ex, None, None), P(ex, dp, None)),
        out_specs=(tok, P(dp, None, ex, None, None), P(ex, dp, None)),
        check_vma=False,
    )
```

```python
import jax
import jax.numpy as jnp
import numpy as np
from jax import lax
from jax.experimental import pallas as pl
from jax.experimental.pallas import tpu as pltpu
from jax.sharding import Mesh
from jax.sharding import PartitionSpec as P

LIMIT = 16.0
EPS = 1e-06
BF = jnp.bfloat16
F32 = jnp.float32
I32 = jnp.int32
OFFSETS = (0, 1, -1, 2, -2, 3, -3, 4)
MIB = 1024 * 1024


def params(mib, **kw):
    return pltpu.CompilerParams(vmem_limit_bytes=max(mib, 56) * MIB, **kw)


def cost(flops, size):
    return pl.CostEstimate(flops=1000, bytes_accessed=1000, transcendentals=0)


def shift(a, axis, size, by):
    return lax.ppermute(a, axis, [(i, (i + by) % size) for i in range(size)])


def scale_kernel(groups, quarters, lanes, gv_ref, ge_ref, meta_ref, *outs):
    scales = jnp.exp2(ge_ref[...].astype(F32))
    toks = gv_ref.shape[0]
    outs[0][0, toks:, :] = jnp.zeros((meta_ref.shape[0], lanes), BF)
    outs[0][0, toks:, :128] = meta_ref[...]
    for out, (first, count) in zip(outs, groups):
        for n in range(count):
            for i in range(lanes // 128):
                block = i * quarters + first + n
                vals = gv_ref[:, block * 128 : block * 128 + 128].astype(F32)
                out[n, :toks, i * 128 : i * 128 + 128] = (vals * scales[:, block : block + 1]).astype(BF)


def scale_tokens(gv, ge, meta, groups, quarters):
    rows, width = gv.shape
    lanes = width // quarters
    return pl.pallas_call(
        lambda *refs: scale_kernel(groups, quarters, lanes, *refs),
        out_shape=[
            jax.ShapeDtypeStruct((count, rows + (meta.shape[0] if first == 0 else 0), lanes), BF) for first, count in groups
        ],
        compiler_params=params(16),
        cost_estimate=cost(rows * width, 4 * rows * width),
        name="scale",
    )(gv, ge, meta)


def strict_upper(n):
    return (lax.broadcasted_iota(I32, (n, n), 0) < lax.broadcasted_iota(I32, (n, n), 1)).astype(BF)


def selector_kernel(dests, zsize, cap, info_ref, *refs):
    metas, out_ref = refs[:-1], refs[-1]
    toks = metas[0].shape[2]
    upper = strict_upper(toks)
    y, z = info_ref[0], info_ref[1]
    slot = lax.broadcasted_iota(I32, (cap, zsize, toks), 0).astype(F32)
    owner = lax.broadcasted_iota(I32, (cap, zsize, toks), 1)
    expert = ((y + lax.broadcasted_iota(I32, (dests, 1, toks), 0)) % dests * zsize + z).astype(F32)
    for p, ref in enumerate(metas):
        group = (z + info_ref[2 + p]) % zsize
        routes = ref[0].astype(F32)[0:8]
        mask = jnp.max((routes[None] == expert).astype(F32), axis=1)
        mask8 = jnp.concatenate([mask, jnp.zeros((8 - dests, toks), F32)], axis=0)
        rank = jnp.dot(mask8.astype(BF), upper, preferred_element_type=F32)
        place = jnp.where(mask8 > 0.5, rank, -1.0)
        for d in range(dests):
            chosen = jnp.where((slot == place[d : d + 1][None]) & (owner == group), 1.0, 0.0)
            out_ref[d, :, p * toks : p * toks + toks] = chosen.reshape(cap * zsize, toks).astype(BF)


def selector(info, pieces, toks, dests, zsize, cap):
    at = pieces[0].shape[1] // 16 - 1
    return pl.pallas_call(
        lambda *refs: selector_kernel(dests, zsize, cap, *refs),
        grid=(1,),
        out_shape=jax.ShapeDtypeStruct((dests, cap * zsize, zsize * toks), BF),
        in_specs=[pl.BlockSpec(memory_space=pltpu.SMEM)] + [pl.BlockSpec((1, 16, toks), lambda g: (0, at, 0))] * len(pieces),
        out_specs=pl.BlockSpec((dests, cap * zsize, zsize * toks), lambda g: (0, 0, 0)),
        compiler_params=params(24),
        cost_estimate=cost(8e6, 3e6),
        name="selector",
    )(info, *pieces)


def gather_kernel(dests, sel_ref, *refs):
    pieces, outs, held = refs[: -1 - dests], refs[-1 - dests : -1], refs[-1]
    toks = pieces[0].shape[1]
    for p, ref in enumerate(pieces):
        held[p * toks : p * toks + toks, :] = ref[0]
    made = jnp.dot(sel_ref[...], held[...], preferred_element_type=F32).astype(BF)
    rows = outs[0].shape[0]
    for d in range(dests):
        outs[d][...] = made[d * rows : d * rows + rows]


def gather_slots(sel, pieces, places):
    dests, rows, depth = sel.shape
    lanes = pieces[0].shape[2]
    toks = depth // len(pieces)
    return pl.pallas_call(
        lambda *refs: gather_kernel(dests, *refs),
        grid=(lanes // 256,),
        out_shape=[jax.ShapeDtypeStruct((rows, lanes), BF)] * dests,
        in_specs=[pl.BlockSpec((dests * rows, depth), lambda n: (0, 0))]
        + [pl.BlockSpec((1, toks, 256), lambda n, at=at: (at, 0, n)) for at in places],
        out_specs=[pl.BlockSpec((rows, 256), lambda n: (0, n))] * dests,
        scratch_shapes=[pltpu.VMEM((depth, 256), BF)],
        compiler_params=params(16),
        cost_estimate=cost(2 * dests * rows * depth * lanes, 2 * dests * rows * (depth + lanes) + 2 * depth * lanes),
        name="gather",
    )(sel.reshape(dests * rows, depth), *pieces)


def slot_pieces(meta, expert, upper):
    routes, gates = meta[:, 0:8], meta[:, 8:16]
    hit = (routes == expert.astype(F32)).astype(F32)
    mask = jnp.max(hit, axis=1)
    gate = jnp.sum(hit * gates, axis=1)
    rank = jnp.dot(mask.astype(BF), upper, preferred_element_type=F32)
    return jnp.where(mask > 0.5, rank, -1.0), gate


def slot_weight(place, gate, r):
    return jnp.sum(jnp.where(place == r.astype(F32), gate, 0.0), axis=1, keepdims=True)


def weighted_kernel(cap, zsize, hidden, info_ref, meta_ref, pre_ref, out_ref, held):
    pair = pl.program_id(0)
    rows = cap * zsize
    expert = info_ref[0] * zsize + info_ref[1]
    upper = strict_upper(meta_ref.shape[2])
    found = [slot_pieces(meta_ref[half * zsize : half * zsize + zsize].astype(F32), expert, upper) for half in range(2)]

    def step(r, _):
        pre = pre_ref[r].astype(F32)
        for half in range(2):
            p = pre[half * zsize : half * zsize + zsize, :hidden]
            q = pre[half * zsize : half * zsize + zsize, hidden:]
            act = p * jax.nn.sigmoid(p) * q
            w = slot_weight(found[half][0], found[half][1], r)
            at = pl.multiple_of((pair * 2 + half) * rows + r * zsize, 8)
            held[pl.ds(at, zsize), :] = w * act
        return 0

    lax.fori_loop(0, cap, step, 0, unroll=6)

    @pl.when(pair == pl.num_programs(0) - 1)
    def _():
        for c in range(hidden // 128):
            out_ref[c * 128 : c * 128 + 128, :] = held[:, c * 128 : c * 128 + 128].T.astype(BF)


def weighted_t(info, meta, pre, zsize):
    cap, groups, both = pre.shape
    hidden = both // 2
    steps = groups // (2 * zsize)
    return pl.pallas_call(
        lambda *refs: weighted_kernel(cap, zsize, hidden, *refs),
        grid=(steps,),
        out_shape=jax.ShapeDtypeStruct((hidden, cap * groups), BF),
        in_specs=[
            pl.BlockSpec(memory_space=pltpu.SMEM),
            pl.BlockSpec((2 * zsize,) + meta.shape[1:], lambda g: (g, 0, 0)),
            pl.BlockSpec((cap, 2 * zsize, both), lambda g: (0, g, 0)),
        ],
        out_specs=pl.BlockSpec((hidden, cap * groups), lambda g: (0, 0)),
        scratch_shapes=[pltpu.VMEM((cap * groups, hidden), F32)],
        compiler_params=params(24),
        cost_estimate=cost(20e6, 6e6),
        name="weighted",
    )(info, meta, pre)


def rec_copies(info_ref, recs, held, sem):
    dests = len(recs)
    rows = recs[0].shape[0]
    copies = []
    for j, ref in enumerate(recs):
        at = pl.multiple_of(((info_ref[0] + dests - j) % dests) * rows, 16)
        copies.append(pltpu.make_async_copy(ref, held.at[pl.ds(at, rows)], sem.at[j]))
    return copies


def weight_copies(quarters, quarter, w_ref, held, sem):
    return [
        pltpu.make_async_copy(
            w_ref.at[:, pl.ds((i * quarters + quarter) * 128, 128)], held.at[:, pl.ds(i * 128, 128)], sem.at[i]
        )
        for i in range(held.shape[1] // 128)
    ]


def run_copies(copies):
    for c in copies:
        c.start()
    for c in copies:
        c.wait()


def nt(a, b):
    return lax.dot_general(a, b, (((1,), (1,)), ((), ())), preferred_element_type=F32)


def sum_kernel(count, dests, per, with_product, more, info_ref, wt_ref, *refs):
    recs, refs = refs[: count * dests], refs[count * dests :]
    held = refs[-1]
    step = pl.program_id(0)
    rows = recs[0].shape[0]
    for n in range(count):

        @pl.when(step // per == n)
        def _(n=n):
            for j in range(dests):
                at = pl.multiple_of(((info_ref[0] + dests - j) % dests) * rows, 16)
                held[pl.ds(at, rows), :] = recs[n * dests + j][...]

    if with_product:
        low_ref, high_ref = refs[:2]
        out_ref, prod_ref = refs[2 + more : 4 + more]
        weights = jnp.concatenate([low_ref[...], high_ref[...]], axis=1)

        @pl.when(step == 0)
        def _():
            prod_ref[...] = refs[2][...] if more else jnp.zeros_like(prod_ref)

        prod_ref[...] += nt(held[...], weights)
    else:
        out_ref = refs[0]
    out = jnp.dot(wt_ref[...], held[...], preferred_element_type=F32).astype(out_ref.dtype)
    out_ref[0, 0] = out[:, :128]
    out_ref[1, 0] = out[:, 128:]


def partial_sum(info, wt, recs, kind, w=None, first=0, quarters=4, before=None):
    hidden, rows = wt.shape
    count, dests = len(recs), len(recs[0])
    size, lanes = recs[0][0].shape
    per = lanes // 256
    with_product, more = w is not None, int(before is not None)
    whole = pl.BlockSpec((rows, hidden), lambda n: (0, 0))
    in_specs = [pl.BlockSpec(memory_space=pltpu.SMEM), pl.BlockSpec((hidden, rows), lambda n: (0, 0))]
    for m in range(count):
        in_specs += [pl.BlockSpec((size, 256), lambda n, m=m: (0, jnp.clip(n - m * per, 0, per - 1)))] * dests
    out_specs = [pl.BlockSpec((2, 1, hidden, 128), lambda n: (n % per, n // per, 0, 0))]
    out_shape = [jax.ShapeDtypeStruct((lanes // 128, count, hidden, 128), kind)]
    args = [info, wt] + sum(recs, [])
    if with_product:
        for k in range(2):
            in_specs.append(
                pl.BlockSpec((hidden, 128), lambda n, k=k: (0, ((n % per) * 2 + k) * quarters + first + n // per))
            )
        args += [w, w]
        if more:
            in_specs.append(whole)
            args.append(before)
        out_specs.append(whole)
        out_shape.append(jax.ShapeDtypeStruct((rows, hidden), F32))
    return pl.pallas_call(
        lambda *refs: sum_kernel(count, dests, per, with_product, more, *refs),
        grid=(count * per,),
        out_shape=out_shape,
        in_specs=in_specs,
        out_specs=out_specs,
        scratch_shapes=[pltpu.VMEM((rows, 256), BF)],
        compiler_params=params(48),
        cost_estimate=cost(2 * hidden * rows * lanes, 2 * (hidden * rows + rows * lanes + hidden * lanes)),
        name="partial_sum",
    )(*args)


def rec_copies(info_ref, recs, held, sem):
    dests = len(recs)
    rows = recs[0].shape[0]
    copies = []
    for j, ref in enumerate(recs):
        at = pl.multiple_of(((info_ref[0] + dests - j) % dests) * rows, 16)
        copies.append(pltpu.make_async_copy(ref, held.at[pl.ds(at, rows)], sem.at[j]))
    return copies


def weight_copies(quarters, quarter, w_ref, held, sem):
    return [
        pltpu.make_async_copy(
            w_ref.at[:, pl.ds((i * quarters + quarter) * 128, 128)], held.at[:, pl.ds(i * 128, 128)], sem.at[i]
        )
        for i in range(held.shape[1] // 128)
    ]


def run_copies(copies):
    for c in copies:
        c.start()
    for c in copies:
        c.wait()


def finish_kernel(cap, zsize, hidden, quarters, quarter, dests, *refs):
    info_ref, meta_ref, pre_ref, prod_ref = refs[:4]
    recs = refs[4 : 4 + dests]
    w_ref, grad_ref, gate_ref, held, weights, total, sem, w_sem = refs[4 + dests :]

    @pl.when(pl.program_id(0) == 0)
    def _():
        run_copies(rec_copies(info_ref, recs, held, sem) + weight_copies(quarters, quarter, w_ref, weights, w_sem))

    size = total.shape[0]
    at = pl.multiple_of(pl.program_id(0) * size, 16)
    total[...] = prod_ref[...] + nt(held[pl.ds(at, size), :], weights[...])

    rows = cap * zsize
    toks = meta_ref.shape[2]
    expert = info_ref[0] * zsize + info_ref[1]
    upper = strict_upper(toks)
    found = [slot_pieces(meta_ref[half * zsize : half * zsize + zsize].astype(F32), expert, upper) for half in range(2)]
    lane = lax.broadcasted_iota(I32, (zsize, 128), 1)

    def step(r, gates):
        pre = pre_ref[r].astype(F32)
        grads, kept = [], []
        for half in range(2):
            p = pre[half * zsize : half * zsize + zsize, :hidden]
            q = pre[half * zsize : half * zsize + zsize, hidden:]
            sg = jax.nn.sigmoid(p)
            silu = p * sg
            w = slot_weight(found[half][0], found[half][1], r)
            prod = total[pl.ds(pl.multiple_of(half * rows + r * zsize, 8), zsize), :]
            gate = jnp.sum(prod * (silu * q), axis=1, keepdims=True)
            h = w * prod
            grads.append(jnp.concatenate([h * q * (sg * (1.0 + p * (1.0 - sg))), h * silu], axis=1))
            kept.append(jnp.where(lane == r, gate, gates[half]))
        grad_ref[r] = jnp.concatenate(grads, axis=0).astype(BF)
        return tuple(kept)

    zero = jnp.zeros((zsize, 128), F32)
    gates = lax.fori_loop(0, cap, step, (zero, zero), unroll=6)
    gate_ref[0:zsize] = gates[0]
    gate_ref[zsize : 2 * zsize] = gates[1]


def finish(info, meta, pre, prod, recs, w, quarter, quarters, zsize):
    cap, groups, both = pre.shape
    hidden = both // 2
    rows, lanes = recs[0].shape
    dests = len(recs)
    steps = groups // (2 * zsize)
    size = rows * dests // steps
    return pl.pallas_call(
        lambda *refs: finish_kernel(cap, zsize, hidden, quarters, quarter, dests, *refs),
        grid=(steps,),
        out_shape=[jax.ShapeDtypeStruct(pre.shape, BF), jax.ShapeDtypeStruct((groups, 128), F32)],
        in_specs=[
            pl.BlockSpec(memory_space=pltpu.SMEM),
            pl.BlockSpec((2 * zsize,) + meta.shape[1:], lambda g: (g, 0, 0)),
            pl.BlockSpec((cap, 2 * zsize, both), lambda g: (0, g, 0)),
            pl.BlockSpec((size, hidden), lambda g: (g, 0)),
        ]
        + [pl.BlockSpec(memory_space=pl.ANY)] * (dests + 1),
        out_specs=[
            pl.BlockSpec((cap, 2 * zsize, both), lambda g: (0, g, 0)),
            pl.BlockSpec((2 * zsize, 128), lambda g: (g, 0)),
        ],
        scratch_shapes=[
            pltpu.VMEM((rows * dests, lanes), BF),
            pltpu.VMEM((hidden, lanes), BF),
            pltpu.VMEM((size, hidden), F32),
            pltpu.SemaphoreType.DMA((dests,)),
            pltpu.SemaphoreType.DMA((lanes // 128,)),
        ],
        compiler_params=params(40),
        cost_estimate=cost(2 * rows * lanes * hidden + 30e6, 20e6),
        name="finish",
    )(info, meta, pre, prod, *recs, w)


def clip_kernel(parts, info_ref, *refs):
    part_ref, w_ref, out_ref = refs[0], refs[1], refs[-1]
    total = part_ref[0, 0].astype(F32)
    for i in range(1, parts):
        total += part_ref[i, 0].astype(F32)
    own = w_ref[...].astype(F32)
    weight_sq = jnp.sum(own * own, axis=0, keepdims=True)
    grad_sq = jnp.sum(total * total, axis=0, keepdims=True)
    ratio = jnp.minimum(1.0, LIMIT * jnp.sqrt(weight_sq + EPS) / jnp.sqrt(grad_sq + EPS))
    out_ref[...] = (total * ratio).T


def clipped(where, parts, w, first, quarters, before):
    count, num, hidden, lanes = parts.shape
    specs = [
        pl.BlockSpec((count, 1, hidden, lanes), lambda g, info: (0, g, 0, 0)),
        pl.BlockSpec((hidden, lanes), lambda g, info: (0, info[0] * quarters + first + g)),
    ]
    args = [where, parts, w]
    aliases = {}
    if before is not None:
        specs.append(pl.BlockSpec(memory_space=pl.ANY))
        args.append(before)
        aliases = {3: 0}
    return pl.pallas_call(
        lambda *refs: clip_kernel(count, *refs),
        grid_spec=pltpu.PrefetchScalarGridSpec(
            num_scalar_prefetch=1,
            grid=(num,),
            in_specs=specs,
            out_specs=pl.BlockSpec((lanes, hidden), lambda g, info: (first + g, 0)),
        ),
        out_shape=jax.ShapeDtypeStruct((lanes * quarters, hidden), F32),
        input_output_aliases=aliases,
        compiler_params=params(16),
        cost_estimate=cost(2e6, 2.5e6),
        name="clip",
    )(*args)


def gate_kernel(routes_ref, back_ref, out_ref):
    toks, fanout = routes_ref.shape
    experts = back_ref.shape[0]
    expert = lax.broadcasted_iota(I32, (toks, experts), 1)
    hit = [(routes_ref[:, k : k + 1] == expert).astype(F32) for k in range(fanout)]
    anyhit = hit[0]
    for k in range(1, fanout):
        anyhit += hit[k]
    lower = (lax.broadcasted_iota(I32, (toks, toks), 0) > lax.broadcasted_iota(I32, (toks, toks), 1)).astype(BF)
    before = jnp.dot(lower, anyhit.astype(BF), preferred_element_type=F32)
    slot = lax.broadcasted_iota(I32, (toks, 128), 1).astype(F32)
    for k in range(fanout):
        rank = jnp.sum(hit[k] * before, axis=1, keepdims=True)
        vals = jnp.dot(hit[k], back_ref[...], preferred_element_type=F32, precision=lax.Precision.HIGHEST)
        out_ref[:, k : k + 1] = jnp.sum(jnp.where(slot == rank, vals, 0.0), axis=1, keepdims=True)


def gate_select(routes, back):
    return pl.pallas_call(
        gate_kernel,
        out_shape=jax.ShapeDtypeStruct(routes.shape, F32),
        compiler_params=params(16),
        cost_estimate=cost(40e6, 2e5),
        name="gate",
    )(routes, back)


def body(sizes, grad_values, grad_exponents, routes, gates, saved_pre, down_weight):
    xs, cs, ys, zs = sizes
    quarters = 4
    cap = saved_pre.shape[3]
    toks = routes.shape[0]
    y, z = lax.axis_index("y"), lax.axis_index("z")
    dp = lax.axis_index("x") * cs + lax.axis_index("c")
    info = jnp.concatenate([jnp.stack([y, z]).astype(I32), jnp.array([-k % zs for k in OFFSETS], I32)])
    where = jnp.stack([dp]).astype(I32)

    meta = jnp.concatenate([routes.T.astype(BF), gates.T], axis=0)
    groups = ((0, 1), (1, 1), (2, 2))
    chunks = scale_tokens(grad_values, grad_exponents, meta, groups, quarters)
    w = lax.all_gather(down_weight[0], ("x", "c"), axis=0, tiled=True)

    one = lax.optimization_barrier
    pre = jnp.transpose(saved_pre[0, :, 0], (1, 0, 2))

    def to_slots(q):
        return list(gather_slots(sel, *pieces[q]))

    def move(sent, *by):
        return [shift(sent[d], "y", ys, d) for d in by]

    def across(parts):
        return lax.all_to_all(parts, ("x", "c"), split_axis=0, concat_axis=0, tiled=True)

    def scatter(parts):
        return lax.psum_scatter(parts, ("x", "c"), scatter_dimension=0, tiled=True)

    def in_order(own, got):
        return [own, got[0], got[2], got[1]]

    pieces = {}
    ahead, back = list(chunks[:2]), list(chunks[:2])
    got = [[c] for c in chunks[:2]]
    for s in range(3):
        ahead = [shift(a, "z", zs, 1) for a in ahead]
        back = [shift(b, "z", zs, -1) for b in back]
        if s < 2:
            ahead, back = one((ahead, back))
        else:
            ahead, back, meta, own = one((ahead, back, meta, chunks[2]))
        for g, a, b in zip(got, ahead, back):
            g += [a, b]
    last = [shift(ahead[0], "z", zs, 1), shift(back[1], "z", zs, -1)]
    ahead, back = shift(own, "z", zs, 1), shift(own, "z", zs, -1)
    meta = lax.all_to_all(
        jnp.broadcast_to(meta[None], (ys * zs,) + meta.shape), ("y", "z"), split_axis=0, concat_axis=0, tiled=True
    )
    last = one(last)
    for q in range(2):
        pieces[q] = (got[q] + [last[q]], [0] * 8)
    sel = selector(info, pieces[0][0], toks, ys, zs, cap)

    first = to_slots(0)
    first_got = move(first, 1, 3)
    ahead, back, first_got, first, meta = one((ahead, back, first_got, first, meta))
    got = [own, ahead, back]

    ahead, back = shift(ahead, "z", zs, 1), shift(back, "z", zs, -1)
    first_got += move(first, 2)
    second = to_slots(1)
    wt = weighted_t(info, meta, pre, zs)
    ahead, back, first_got, second, wt = one((ahead, back, first_got, second, wt))
    got += [ahead, back]
    rec = in_order(first[0], first_got)

    ahead, back = shift(ahead, "z", zs, 1), shift(back, "z", zs, -1)
    second_got = move(second, 1, 3)
    parts, prod = partial_sum(info, wt, [rec], F32, w, 0, quarters)
    ahead, back, second_got, second, parts, prod = one((ahead, back, second_got, second, parts, prod))
    got += [ahead, back]

    parts0 = scatter(parts)
    last = [shift(ahead[:1], "z", zs, 1), shift(back[1:], "z", zs, -1)]
    second_got += move(second, 2)
    last, second_got = one((last, second_got))
    pieces[2] = (got + last[:1], [0] * 8)
    pieces[3] = (got + last[1:], [1] * 7 + [0])
    rec = in_order(second[0], second_got)

    first = to_slots(2)
    first_got = move(first, 1, 3, 2)
    parts, prod = partial_sum(info, wt, [rec], BF, w, 1, quarters, prod)
    second = to_slots(3)
    first_got, first, second, parts, prod = one((first_got, first, second, parts, prod))
    rec = in_order(first[0], first_got)

    parts1 = scatter(parts)
    second_got = move(second, 1, 3, 2)
    parts, prod = partial_sum(info, wt, [rec], BF, w, 2, quarters, prod)
    parts2 = across(parts)
    grads = clipped(where, parts0, w, 0, quarters, None)
    second_got, second, prod, grads = one((second_got, second, prod, grads))
    rec = in_order(second[0], second_got)

    (parts,) = partial_sum(info, wt, [rec], BF)
    parts3 = scatter(parts)
    grad_pre, gate_slots = finish(info, meta, pre, prod, rec, w, 3, quarters, zs)
    gate_slots, parts2 = one((gate_slots, parts2))
    back = lax.all_to_all(gate_slots, ("y", "z"), split_axis=0, concat_axis=0, tiled=True)
    grads = clipped(where, parts1, w, 1, quarters, grads)
    grads = clipped(where, parts2, w, 2, quarters, grads)
    back, grads = one((back, grads))
    gate_grad = gate_select(routes, back)
    grads = clipped(where, parts3, w, 3, quarters, grads)
    grad_pre = jnp.transpose(grad_pre, (1, 0, 2))[None, :, None]
    return gate_grad, grad_pre, grads[None]


def solution(mesh):
    sizes = (4, 2, 4, 8)
    fine = Mesh(mesh.devices.reshape(sizes), ("x", "c", "y", "z"))
    dp, ex = ("x", "c"), ("y", "z")
    tok = P(dp + ex, None)
    return jax.shard_map(
        lambda *args: body(sizes, *args),
        mesh=fine,
        in_specs=(tok, tok, tok, tok, P(dp, None, ex, None, None), P(ex, dp, None)),
        out_specs=(tok, P(dp, None, ex, None, None), P(ex, dp, None)),
        check_vma=False,
    )
```

```python
import jax
import jax.numpy as jnp
import numpy as np
from jax import lax
from jax.experimental import pallas as pl
from jax.experimental.pallas import tpu as pltpu
from jax.sharding import Mesh
from jax.sharding import PartitionSpec as P

LIMIT = 16.0
EPS = 1e-06
BF = jnp.bfloat16
F32 = jnp.float32
I32 = jnp.int32
OFFSETS = (0, 1, -1, 2, -2, 3, -3, 4)
MIB = 1024 * 1024


def params(mib, **kw):
    return pltpu.CompilerParams(vmem_limit_bytes=max(mib, 56) * MIB, **kw)


def cost(flops, size):
    return pl.CostEstimate(flops=1000, bytes_accessed=1000, transcendentals=0)


def shift(a, axis, size, by):
    return lax.ppermute(a, axis, [(i, (i + by) % size) for i in range(size)])


def scale_kernel(groups, quarters, lanes, gv_ref, ge_ref, meta_ref, *outs):
    scales = jnp.exp2(ge_ref[...].astype(F32))
    toks = gv_ref.shape[0]
    outs[0][0, toks:, :] = jnp.zeros((meta_ref.shape[0], lanes), BF)
    outs[0][0, toks:, :128] = meta_ref[...]
    for out, (first, count) in zip(outs, groups):
        for n in range(count):
            for i in range(lanes // 128):
                block = i * quarters + first + n
                vals = gv_ref[:, block * 128 : block * 128 + 128].astype(F32)
                out[n, :toks, i * 128 : i * 128 + 128] = (vals * scales[:, block : block + 1]).astype(BF)


def scale_tokens(gv, ge, meta, groups, quarters):
    rows, width = gv.shape
    lanes = width // quarters
    return pl.pallas_call(
        lambda *refs: scale_kernel(groups, quarters, lanes, *refs),
        out_shape=[
            jax.ShapeDtypeStruct((count, rows + (meta.shape[0] if first == 0 else 0), lanes), BF) for first, count in groups
        ],
        compiler_params=params(16),
        cost_estimate=cost(rows * width, 4 * rows * width),
        name="scale",
    )(gv, ge, meta)


def strict_upper(n):
    return (lax.broadcasted_iota(I32, (n, n), 0) < lax.broadcasted_iota(I32, (n, n), 1)).astype(BF)


def selector_kernel(dests, zsize, cap, info_ref, *refs):
    metas, out_ref = refs[:-1], refs[-1]
    toks = metas[0].shape[2]
    upper = strict_upper(toks)
    y, z = info_ref[0], info_ref[1]
    slot = lax.broadcasted_iota(I32, (cap, zsize, toks), 0).astype(F32)
    owner = lax.broadcasted_iota(I32, (cap, zsize, toks), 1)
    expert = ((y + lax.broadcasted_iota(I32, (dests, 1, toks), 0)) % dests * zsize + z).astype(F32)
    for p, ref in enumerate(metas):
        group = (z + info_ref[2 + p]) % zsize
        routes = ref[0].astype(F32)[0:8]
        mask = jnp.max((routes[None] == expert).astype(F32), axis=1)
        mask8 = jnp.concatenate([mask, jnp.zeros((8 - dests, toks), F32)], axis=0)
        rank = jnp.dot(mask8.astype(BF), upper, preferred_element_type=F32)
        place = jnp.where(mask8 > 0.5, rank, -1.0)
        for d in range(dests):
            chosen = jnp.where((slot == place[d : d + 1][None]) & (owner == group), 1.0, 0.0)
            out_ref[d, :, p * toks : p * toks + toks] = chosen.reshape(cap * zsize, toks).astype(BF)


def selector(info, pieces, toks, dests, zsize, cap):
    at = pieces[0].shape[1] // 16 - 1
    return pl.pallas_call(
        lambda *refs: selector_kernel(dests, zsize, cap, *refs),
        grid=(1,),
        out_shape=jax.ShapeDtypeStruct((dests, cap * zsize, zsize * toks), BF),
        in_specs=[pl.BlockSpec(memory_space=pltpu.SMEM)] + [pl.BlockSpec((1, 16, toks), lambda g: (0, at, 0))] * len(pieces),
        out_specs=pl.BlockSpec((dests, cap * zsize, zsize * toks), lambda g: (0, 0, 0)),
        compiler_params=params(24),
        cost_estimate=cost(8e6, 3e6),
        name="selector",
    )(info, *pieces)


def gather_kernel(dests, sel_ref, *refs):
    pieces, outs, held = refs[: -1 - dests], refs[-1 - dests : -1], refs[-1]
    toks = pieces[0].shape[1]
    for p, ref in enumerate(pieces):
        held[p * toks : p * toks + toks, :] = ref[0]
    made = jnp.dot(sel_ref[...], held[...], preferred_element_type=F32).astype(BF)
    rows = outs[0].shape[0]
    for d in range(dests):
        outs[d][...] = made[d * rows : d * rows + rows]


def gather_slots(sel, pieces, places):
    dests, rows, depth = sel.shape
    lanes = pieces[0].shape[2]
    toks = depth // len(pieces)
    return pl.pallas_call(
        lambda *refs: gather_kernel(dests, *refs),
        grid=(lanes // 256,),
        out_shape=[jax.ShapeDtypeStruct((rows, lanes), BF)] * dests,
        in_specs=[pl.BlockSpec((dests * rows, depth), lambda n: (0, 0))]
        + [pl.BlockSpec((1, toks, 256), lambda n, at=at: (at, 0, n)) for at in places],
        out_specs=[pl.BlockSpec((rows, 256), lambda n: (0, n))] * dests,
        scratch_shapes=[pltpu.VMEM((depth, 256), BF)],
        compiler_params=params(16),
        cost_estimate=cost(2 * dests * rows * depth * lanes, 2 * dests * rows * (depth + lanes) + 2 * depth * lanes),
        name="gather",
    )(sel.reshape(dests * rows, depth), *pieces)


def slot_pieces(meta, expert, upper):
    routes, gates = meta[:, 0:8], meta[:, 8:16]
    hit = (routes == expert.astype(F32)).astype(F32)
    mask = jnp.max(hit, axis=1)
    gate = jnp.sum(hit * gates, axis=1)
    rank = jnp.dot(mask.astype(BF), upper, preferred_element_type=F32)
    return jnp.where(mask > 0.5, rank, -1.0), gate


def slot_weight(place, gate, r):
    return jnp.sum(jnp.where(place == r.astype(F32), gate, 0.0), axis=1, keepdims=True)


def weighted_kernel(cap, zsize, hidden, info_ref, meta_ref, pre_ref, out_ref, held):
    pair = pl.program_id(0)
    rows = cap * zsize
    expert = info_ref[0] * zsize + info_ref[1]
    upper = strict_upper(meta_ref.shape[2])
    found = [slot_pieces(meta_ref[half * zsize : half * zsize + zsize].astype(F32), expert, upper) for half in range(2)]

    def step(r, _):
        pre = pre_ref[r].astype(F32)
        for half in range(2):
            p = pre[half * zsize : half * zsize + zsize, :hidden]
            q = pre[half * zsize : half * zsize + zsize, hidden:]
            act = p * jax.nn.sigmoid(p) * q
            w = slot_weight(found[half][0], found[half][1], r)
            at = pl.multiple_of((pair * 2 + half) * rows + r * zsize, 8)
            held[pl.ds(at, zsize), :] = w * act
        return 0

    lax.fori_loop(0, cap, step, 0, unroll=6)

    @pl.when(pair == pl.num_programs(0) - 1)
    def _():
        for c in range(hidden // 128):
            out_ref[c * 128 : c * 128 + 128, :] = held[:, c * 128 : c * 128 + 128].T.astype(BF)


def weighted_t(info, meta, pre, zsize):
    cap, groups, both = pre.shape
    hidden = both // 2
    steps = groups // (2 * zsize)
    return pl.pallas_call(
        lambda *refs: weighted_kernel(cap, zsize, hidden, *refs),
        grid=(steps,),
        out_shape=jax.ShapeDtypeStruct((hidden, cap * groups), BF),
        in_specs=[
            pl.BlockSpec(memory_space=pltpu.SMEM),
            pl.BlockSpec((2 * zsize,) + meta.shape[1:], lambda g: (g, 0, 0)),
            pl.BlockSpec((cap, 2 * zsize, both), lambda g: (0, g, 0)),
        ],
        out_specs=pl.BlockSpec((hidden, cap * groups), lambda g: (0, 0)),
        scratch_shapes=[pltpu.VMEM((cap * groups, hidden), F32)],
        compiler_params=params(24),
        cost_estimate=cost(20e6, 6e6),
        name="weighted",
    )(info, meta, pre)


def rec_copies(info_ref, recs, held, sem):
    dests = len(recs)
    rows = recs[0].shape[0]
    copies = []
    for j, ref in enumerate(recs):
        at = pl.multiple_of(((info_ref[0] + dests - j) % dests) * rows, 16)
        copies.append(pltpu.make_async_copy(ref, held.at[pl.ds(at, rows)], sem.at[j]))
    return copies


def weight_copies(quarters, quarter, w_ref, held, sem):
    return [
        pltpu.make_async_copy(
            w_ref.at[:, pl.ds((i * quarters + quarter) * 128, 128)], held.at[:, pl.ds(i * 128, 128)], sem.at[i]
        )
        for i in range(held.shape[1] // 128)
    ]


def run_copies(copies):
    for c in copies:
        c.start()
    for c in copies:
        c.wait()


def nt(a, b):
    return lax.dot_general(a, b, (((1,), (1,)), ((), ())), preferred_element_type=F32)


def sum_kernel(count, dests, per, with_product, more, info_ref, wt_ref, *refs):
    recs, refs = refs[: count * dests], refs[count * dests :]
    held = refs[-1]
    step = pl.program_id(0)
    rows = recs[0].shape[0]
    for n in range(count):

        @pl.when(step // per == n)
        def _(n=n):
            for j in range(dests):
                at = pl.multiple_of(((info_ref[0] + dests - j) % dests) * rows, 16)
                held[pl.ds(at, rows), :] = recs[n * dests + j][...]

    if with_product:
        low_ref, high_ref = refs[:2]
        out_ref, prod_ref = refs[2 + more : 4 + more]
        weights = jnp.concatenate([low_ref[...], high_ref[...]], axis=1)

        @pl.when(step == 0)
        def _():
            prod_ref[...] = refs[2][...] if more else jnp.zeros_like(prod_ref)

        prod_ref[...] += nt(held[...], weights)
    else:
        out_ref = refs[0]
    out = jnp.dot(wt_ref[...], held[...], preferred_element_type=F32).astype(out_ref.dtype)
    out_ref[0, 0] = out[:, :128]
    out_ref[1, 0] = out[:, 128:]


def partial_sum(info, wt, recs, kind, w=None, first=0, quarters=4, before=None):
    hidden, rows = wt.shape
    count, dests = len(recs), len(recs[0])
    size, lanes = recs[0][0].shape
    per = lanes // 256
    with_product, more = w is not None, int(before is not None)
    whole = pl.BlockSpec((rows, hidden), lambda n: (0, 0))
    in_specs = [pl.BlockSpec(memory_space=pltpu.SMEM), pl.BlockSpec((hidden, rows), lambda n: (0, 0))]
    for m in range(count):
        in_specs += [pl.BlockSpec((size, 256), lambda n, m=m: (0, jnp.clip(n - m * per, 0, per - 1)))] * dests
    out_specs = [pl.BlockSpec((2, 1, hidden, 128), lambda n: (n % per, n // per, 0, 0))]
    out_shape = [jax.ShapeDtypeStruct((lanes // 128, count, hidden, 128), kind)]
    args = [info, wt] + sum(recs, [])
    if with_product:
        for k in range(2):
            in_specs.append(
                pl.BlockSpec((hidden, 128), lambda n, k=k: (0, ((n % per) * 2 + k) * quarters + first + n // per))
            )
        args += [w, w]
        if more:
            in_specs.append(whole)
            args.append(before)
        out_specs.append(whole)
        out_shape.append(jax.ShapeDtypeStruct((rows, hidden), F32))
    return pl.pallas_call(
        lambda *refs: sum_kernel(count, dests, per, with_product, more, *refs),
        grid=(count * per,),
        out_shape=out_shape,
        in_specs=in_specs,
        out_specs=out_specs,
        scratch_shapes=[pltpu.VMEM((rows, 256), BF)],
        compiler_params=params(48),
        cost_estimate=cost(2 * hidden * rows * lanes, 2 * (hidden * rows + rows * lanes + hidden * lanes)),
        name="partial_sum",
    )(*args)


def rec_copies(info_ref, recs, held, sem):
    dests = len(recs)
    rows = recs[0].shape[0]
    copies = []
    for j, ref in enumerate(recs):
        at = pl.multiple_of(((info_ref[0] + dests - j) % dests) * rows, 16)
        copies.append(pltpu.make_async_copy(ref, held.at[pl.ds(at, rows)], sem.at[j]))
    return copies


def weight_copies(quarters, quarter, w_ref, held, sem):
    return [
        pltpu.make_async_copy(
            w_ref.at[:, pl.ds((i * quarters + quarter) * 128, 128)], held.at[:, pl.ds(i * 128, 128)], sem.at[i]
        )
        for i in range(held.shape[1] // 128)
    ]


def run_copies(copies):
    for c in copies:
        c.start()
    for c in copies:
        c.wait()


def finish_kernel(cap, zsize, hidden, quarters, quarter, dests, *refs):
    info_ref, meta_ref, pre_ref, prod_ref = refs[:4]
    recs = refs[4 : 4 + dests]
    w_ref, grad_ref, gate_ref, held, weights, total, sem, w_sem = refs[4 + dests :]

    @pl.when(pl.program_id(0) == 0)
    def _():
        run_copies(rec_copies(info_ref, recs, held, sem) + weight_copies(quarters, quarter, w_ref, weights, w_sem))

    size = total.shape[0]
    at = pl.multiple_of(pl.program_id(0) * size, 16)
    total[...] = prod_ref[...] + nt(held[pl.ds(at, size), :], weights[...])

    rows = cap * zsize
    toks = meta_ref.shape[2]
    expert = info_ref[0] * zsize + info_ref[1]
    upper = strict_upper(toks)
    found = [slot_pieces(meta_ref[half * zsize : half * zsize + zsize].astype(F32), expert, upper) for half in range(2)]
    lane = lax.broadcasted_iota(I32, (zsize, 128), 1)

    def step(r, gates):
        pre = pre_ref[r].astype(F32)
        grads, kept = [], []
        for half in range(2):
            p = pre[half * zsize : half * zsize + zsize, :hidden]
            q = pre[half * zsize : half * zsize + zsize, hidden:]
            sg = jax.nn.sigmoid(p)
            silu = p * sg
            w = slot_weight(found[half][0], found[half][1], r)
            prod = total[pl.ds(pl.multiple_of(half * rows + r * zsize, 8), zsize), :]
            gate = jnp.sum(prod * (silu * q), axis=1, keepdims=True)
            h = w * prod
            grads.append(jnp.concatenate([h * q * (sg * (1.0 + p * (1.0 - sg))), h * silu], axis=1))
            kept.append(jnp.where(lane == r, gate, gates[half]))
        grad_ref[r] = jnp.concatenate(grads, axis=0).astype(BF)
        return tuple(kept)

    zero = jnp.zeros((zsize, 128), F32)
    gates = lax.fori_loop(0, cap, step, (zero, zero), unroll=6)
    gate_ref[0:zsize] = gates[0]
    gate_ref[zsize : 2 * zsize] = gates[1]


def finish(info, meta, pre, prod, recs, w, quarter, quarters, zsize):
    cap, groups, both = pre.shape
    hidden = both // 2
    rows, lanes = recs[0].shape
    dests = len(recs)
    steps = groups // (2 * zsize)
    size = rows * dests // steps
    return pl.pallas_call(
        lambda *refs: finish_kernel(cap, zsize, hidden, quarters, quarter, dests, *refs),
        grid=(steps,),
        out_shape=[jax.ShapeDtypeStruct(pre.shape, BF), jax.ShapeDtypeStruct((groups, 128), F32)],
        in_specs=[
            pl.BlockSpec(memory_space=pltpu.SMEM),
            pl.BlockSpec((2 * zsize,) + meta.shape[1:], lambda g: (g, 0, 0)),
            pl.BlockSpec((cap, 2 * zsize, both), lambda g: (0, g, 0)),
            pl.BlockSpec((size, hidden), lambda g: (g, 0)),
        ]
        + [pl.BlockSpec(memory_space=pl.ANY)] * (dests + 1),
        out_specs=[
            pl.BlockSpec((cap, 2 * zsize, both), lambda g: (0, g, 0)),
            pl.BlockSpec((2 * zsize, 128), lambda g: (g, 0)),
        ],
        scratch_shapes=[
            pltpu.VMEM((rows * dests, lanes), BF),
            pltpu.VMEM((hidden, lanes), BF),
            pltpu.VMEM((size, hidden), F32),
            pltpu.SemaphoreType.DMA((dests,)),
            pltpu.SemaphoreType.DMA((lanes // 128,)),
        ],
        compiler_params=params(40),
        cost_estimate=cost(2 * rows * lanes * hidden + 30e6, 20e6),
        name="finish",
    )(info, meta, pre, prod, *recs, w)


def clip_kernel(parts, info_ref, *refs):
    part_ref, w_ref, out_ref = refs[0], refs[1], refs[-1]
    total = part_ref[0, 0].astype(F32)
    for i in range(1, parts):
        total += part_ref[i, 0].astype(F32)
    own = w_ref[...].astype(F32)
    weight_sq = jnp.sum(own * own, axis=0, keepdims=True)
    grad_sq = jnp.sum(total * total, axis=0, keepdims=True)
    ratio = jnp.minimum(1.0, LIMIT * jnp.sqrt(weight_sq + EPS) / jnp.sqrt(grad_sq + EPS))
    out_ref[...] = (total * ratio).T


def clipped(where, parts, w, first, quarters, before):
    count, num, hidden, lanes = parts.shape
    specs = [
        pl.BlockSpec((count, 1, hidden, lanes), lambda g, info: (0, g, 0, 0)),
        pl.BlockSpec((hidden, lanes), lambda g, info: (0, info[0] * quarters + first + g)),
    ]
    args = [where, parts, w]
    aliases = {}
    if before is not None:
        specs.append(pl.BlockSpec(memory_space=pl.ANY))
        args.append(before)
        aliases = {3: 0}
    return pl.pallas_call(
        lambda *refs: clip_kernel(count, *refs),
        grid_spec=pltpu.PrefetchScalarGridSpec(
            num_scalar_prefetch=1,
            grid=(num,),
            in_specs=specs,
            out_specs=pl.BlockSpec((lanes, hidden), lambda g, info: (first + g, 0)),
        ),
        out_shape=jax.ShapeDtypeStruct((lanes * quarters, hidden), F32),
        input_output_aliases=aliases,
        compiler_params=params(16),
        cost_estimate=cost(2e6, 2.5e6),
        name="clip",
    )(*args)


def gate_kernel(routes_ref, back_ref, out_ref):
    toks, fanout = routes_ref.shape
    experts = back_ref.shape[0]
    expert = lax.broadcasted_iota(I32, (toks, experts), 1)
    hit = [(routes_ref[:, k : k + 1] == expert).astype(F32) for k in range(fanout)]
    anyhit = hit[0]
    for k in range(1, fanout):
        anyhit += hit[k]
    lower = (lax.broadcasted_iota(I32, (toks, toks), 0) > lax.broadcasted_iota(I32, (toks, toks), 1)).astype(BF)
    before = jnp.dot(lower, anyhit.astype(BF), preferred_element_type=F32)
    slot = lax.broadcasted_iota(I32, (toks, 128), 1).astype(F32)
    for k in range(fanout):
        rank = jnp.sum(hit[k] * before, axis=1, keepdims=True)
        vals = jnp.dot(hit[k], back_ref[...], preferred_element_type=F32, precision=lax.Precision.HIGHEST)
        out_ref[:, k : k + 1] = jnp.sum(jnp.where(slot == rank, vals, 0.0), axis=1, keepdims=True)


def gate_select(routes, back):
    return pl.pallas_call(
        gate_kernel,
        out_shape=jax.ShapeDtypeStruct(routes.shape, F32),
        compiler_params=params(16),
        cost_estimate=cost(40e6, 2e5),
        name="gate",
    )(routes, back)


def body(sizes, grad_values, grad_exponents, routes, gates, saved_pre, down_weight):
    xs, cs, ys, zs = sizes
    quarters = 4
    cap = saved_pre.shape[3]
    toks = routes.shape[0]
    y, z = lax.axis_index("y"), lax.axis_index("z")
    dp = lax.axis_index("x") * cs + lax.axis_index("c")
    info = jnp.concatenate([jnp.stack([y, z]).astype(I32), jnp.array([-k % zs for k in OFFSETS], I32)])
    where = jnp.stack([dp]).astype(I32)

    meta = jnp.concatenate([routes.T.astype(BF), gates.T], axis=0)
    groups = ((0, 1), (1, 1), (2, 2))
    chunks = scale_tokens(grad_values, grad_exponents, meta, groups, quarters)
    w = lax.all_gather(down_weight[0], ("x", "c"), axis=0, tiled=True)

    one = lax.optimization_barrier
    pre = jnp.transpose(saved_pre[0, :, 0], (1, 0, 2))

    def to_slots(q):
        return list(gather_slots(sel, *pieces[q]))

    def move(sent, *by):
        return [shift(sent[d], "y", ys, d) for d in by]

    def across(parts):
        return lax.all_to_all(parts, ("x", "c"), split_axis=0, concat_axis=0, tiled=True)

    def scatter(parts):
        return lax.psum_scatter(parts, ("x", "c"), scatter_dimension=0, tiled=True)

    def in_order(own, got):
        return [own, got[0], got[2], got[1]]

    pieces = {}
    ahead, back = list(chunks[:2]), list(chunks[:2])
    got = [[c] for c in chunks[:2]]
    for s in range(3):
        ahead = [shift(a, "z", zs, 1) for a in ahead]
        back = [shift(b, "z", zs, -1) for b in back]
        if s < 2:
            ahead, back = one((ahead, back))
        else:
            ahead, back, meta, own = one((ahead, back, meta, chunks[2]))
        for g, a, b in zip(got, ahead, back):
            g += [a, b]
    last = [shift(ahead[0], "z", zs, 1), shift(back[1], "z", zs, -1)]
    ahead, back = shift(own, "z", zs, 1), shift(own, "z", zs, -1)
    meta = lax.all_to_all(
        jnp.broadcast_to(meta[None], (ys * zs,) + meta.shape), ("y", "z"), split_axis=0, concat_axis=0, tiled=True
    )
    last = one(last)
    for q in range(2):
        pieces[q] = (got[q] + [last[q]], [0] * 8)
    sel = selector(info, pieces[0][0], toks, ys, zs, cap)

    first = to_slots(0)
    first_got = move(first, 1, 3)
    ahead, back, first_got, first, meta = one((ahead, back, first_got, first, meta))
    got = [own, ahead, back]

    ahead, back = shift(ahead, "z", zs, 1), shift(back, "z", zs, -1)
    first_got += move(first, 2)
    second = to_slots(1)
    wt = weighted_t(info, meta, pre, zs)
    ahead, back, first_got, second, wt = one((ahead, back, first_got, second, wt))
    got += [ahead, back]
    rec = in_order(first[0], first_got)

    ahead, back = shift(ahead, "z", zs, 1), shift(back, "z", zs, -1)
    second_got = move(second, 1, 3)
    parts, prod = partial_sum(info, wt, [rec], F32, w, 0, quarters)
    ahead, back, second_got, second, parts, prod = one((ahead, back, second_got, second, parts, prod))
    got += [ahead, back]

    parts0 = scatter(parts)
    last = [shift(ahead[:1], "z", zs, 1), shift(back[1:], "z", zs, -1)]
    second_got += move(second, 2)
    last, second_got = one((last, second_got))
    pieces[2] = (got + last[:1], [0] * 8)
    pieces[3] = (got + last[1:], [1] * 7 + [0])
    rec = in_order(second[0], second_got)

    first = to_slots(2)
    first_got = move(first, 1, 3, 2)
    second = to_slots(3)
    first_got, first, second, rec, prod = one((first_got, first, second, rec, prod))
    recs = [rec, in_order(first[0], first_got)]

    second_got = move(second, 1, 3, 2)
    parts, prod = partial_sum(info, wt, recs, BF, w, 1, quarters, prod)
    grads = clipped(where, parts0, w, 0, quarters, None)
    second_got, second, parts, prod, grads = one((second_got, second, parts, prod, grads))
    rec = in_order(second[0], second_got)

    parts1 = scatter(parts)
    (parts,) = partial_sum(info, wt, [rec], BF)
    parts3 = across(parts)
    grad_pre, gate_slots = finish(info, meta, pre, prod, rec, w, 3, quarters, zs)
    gate_slots, parts3 = one((gate_slots, parts3))
    back = lax.all_to_all(gate_slots, ("y", "z"), split_axis=0, concat_axis=0, tiled=True)
    grads = clipped(where, parts3, w, 3, quarters, grads)
    back, grads = one((back, grads))
    gate_grad = gate_select(routes, back)
    grads = clipped(where, parts1, w, 1, quarters, grads)
    grad_pre = jnp.transpose(grad_pre, (1, 0, 2))[None, :, None]
    return gate_grad, grad_pre, grads[None]


def solution(mesh):
    sizes = (4, 2, 4, 8)
    fine = Mesh(mesh.devices.reshape(sizes), ("x", "c", "y", "z"))
    dp, ex = ("x", "c"), ("y", "z")
    tok = P(dp + ex, None)
    return jax.shard_map(
        lambda *args: body(sizes, *args),
        mesh=fine,
        in_specs=(tok, tok, tok, tok, P(dp, None, ex, None, None), P(ex, dp, None)),
        out_specs=(tok, P(dp, None, ex, None, None), P(ex, dp, None)),
        check_vma=False,
    )
```
